32 devices in a mesh: wide: 4 (over y, x), perm: 8 (over z, core).
Axes of the slice: x: 2, y: 2, z: 4, core: 2. Of those that a mesh axis runs over, the one named last changes fastest.
Arguments:
- amplitudes: bfloat16 [16, 2048, 2048], P('wide', 'perm'), may hold values from -6 to 6
- integrals: bfloat16 [2048, 2048], P('perm'), may hold values from -0.125 to 0.125
- coupling: float32 [16, 9], replicated, may hold values from -2 to 2
- pair_energy: float32 [16], P('wide'), may hold values from -2 to -0.5
- virtual_energy: float32 [2048], replicated, may hold values from 0.5 to 3
- tile_sizes: int32 [16], replicated, may hold values from 64 to 128, as said below
- blocks: int32 [16, 16, 16], P('wide'), may hold values 0 or 1
Outputs:
- update: bfloat16 [16, 2048, 2048], P('wide', 'perm')
The draws below stay inside these ranges and needn't reach their ends.
Inputs may be any that keep to these rules, and one draw needn't show every extreme that they name: `tile_sizes`: some tile has 128 live slots and some tile 128 // 2.
All inputs are finite; a program needn't handle non-finite values. No bound on the sum of `blocks` on one device may be relied on, other than what follows from the above.
Results may differ from the reference program's by a relative error of at most 0.0058.
Values may be sent and summed in bfloat16 or wider, within the bound.
A program may use at most 128 MiB of HBM per device.

```python
import jax
import jax.numpy as jnp
from jax import lax

NV = 2048
TS = 128
BAND = 4
NT = 16
P_SIZE = 16


def draw_tile_sizes(key, part):
    first, second = jax.random.split(key)
    sizes = jax.random.randint(first, (NT,), TS // 2, TS + 1)
    order = jax.random.permutation(second, NT)
    sizes = sizes.at[order[0]].set(TS).at[order[1]].set(TS // 2)
    return sizes.astype(jnp.int32)


def set_ends(result, own_key, low, high):
    place = [jax.random.randint(jax.random.fold_in(own_key, axis), (), 0, length) for axis, length in enumerate(result.shape)]
    widest = result.shape.index(max(result.shape))
    neighbour = place[:widest] + [(place[widest] + 1) % result.shape[widest]] + place[widest + 1:]
    return result.at[tuple(place)].set(low).at[tuple(neighbour)].set(high)


def level_of(rng, extent, pieces, low, largest):
    loudness = 1.0
    for position, blocks in pieces:
        heights = jax.random.uniform(jax.random.fold_in(jax.random.fold_in(rng, 6), position), (blocks,), jnp.float32, low / len(pieces), largest / len(pieces))
        loudness = loudness * jnp.repeat(jnp.exp(heights), extent[position] // blocks).reshape((-1,) + (1,) * (len(extent) - 1 - position))
    return loudness


def normal_values(key, dims, scale, bound, shards=(), held_as=jnp.bfloat16):
    entries = scale * jax.random.normal(key, dims, jnp.float32)
    if shards:
        entries = entries * level_of(key, dims, shards, -0.22, 0.18)
    return jnp.clip(entries, -bound, bound).astype(held_as)


def setup_inputs(seed: int = 0) -> dict:
    key_of = jax.random.split(jax.random.key(seed), 8)
    amplitudes = normal_values(key_of[0], (P_SIZE, NV, NV), 1.0, 6.0, ((0, 4), (1, 8)))
    integrals = normal_values(key_of[1], (NV, NV), NV ** -0.5, 0.125, ((0, 8),))
    coupling = normal_values(key_of[2], (P_SIZE, 2 * BAND + 1), 0.35, 2.0, (), jnp.float32)
    pair_energy = jnp.clip(-2.0 + 1.5 * jax.random.uniform(key_of[3], (P_SIZE,), jnp.float32) ** level_of(key_of[3], (P_SIZE,), ((0, 4),), -0.2, 0.2), -2.0, -0.5)
    virtual_energy = jnp.clip(jax.random.uniform(key_of[4], (NV,), jnp.float32, 0.5, 3.0), 0.5, 3.0)
    tile_sizes = draw_tile_sizes(jax.random.fold_in(key_of[7], 71), 0)
    blocks = set_ends((jax.random.randint(key_of[6], (P_SIZE, NT, NT), 0, 3) < 2).astype(jnp.int32), jax.random.fold_in(key_of[6], 1), 0, 1)
    return {"amplitudes": amplitudes, "integrals": integrals, "coupling": coupling, "pair_energy": pair_energy, "virtual_energy": virtual_energy, "tile_sizes": tile_sizes, "blocks": blocks}


def reference(amplitudes, integrals, coupling, pair_energy, virtual_energy, tile_sizes, blocks):
    total_pairs = amplitudes.shape[0]
    width = amplitudes.shape[1]
    tile_count = tile_sizes.shape[0]
    slot_size = width // tile_count
    reach = (coupling.shape[1] - 1) // 2
    live_all = (jnp.arange(slot_size, dtype=jnp.int32)[None, :] < tile_sizes[:, None]).reshape(width).astype(jnp.float32)

    def one_pair(index):
        mixed = jnp.zeros((width, width), jnp.float32)
        for offset in range(2 * reach + 1):
            source = index + offset - reach
            valid = (source >= 0) & (source < total_pairs)
            clipped = jnp.clip(source, 0, total_pairs - 1).astype(jnp.int32)
            slab = lax.dynamic_index_in_dim(amplitudes, clipped, 0, keepdims=False).astype(jnp.float32)
            weight = jnp.where(valid, coupling[index, offset], jnp.float32(0.0))
            mixed = mixed + weight * slab
        cycle = jnp.dot(mixed.astype(jnp.bfloat16), integrals, preferred_element_type=jnp.float32).astype(jnp.bfloat16)
        cycle = lax.optimization_barrier(cycle)
        cycle_wide = cycle.astype(jnp.float32)
        residual = cycle_wide + cycle_wide.T
        pattern = lax.dynamic_index_in_dim(blocks, index, 0, keepdims=False).astype(jnp.float32)
        pattern = jnp.repeat(jnp.repeat(pattern, slot_size, axis=0), slot_size, axis=1)
        mask = pattern * live_all[:, None] * live_all[None, :]
        denom = virtual_energy[:, None] + virtual_energy[None, :] - pair_energy[index]
        return (mask * (residual / denom)).astype(jnp.bfloat16)

    return lax.map(one_pair, jnp.arange(total_pairs, dtype=jnp.int32))
```

```python
import functools

import jax
import jax.numpy as jnp
from jax import lax
from jax.experimental import pallas as pl
from jax.experimental.pallas import tpu as pltpu
from jax.sharding import PartitionSpec as P

VMEM_BYTES = 48 * 1024 * 1024


def share_kernel(target_of, i, coupling_ref, amp_ref, *refs):
    pairs = amp_ref.shape[0]
    total_pairs, offsets = coupling_ref.shape
    source = lax.axis_index("wide")
    target, wanted = target_of(source)
    row = target * pairs + i
    total = None
    for j in range(pairs):
        k = (source - target) * pairs + j - i + (offsets - 1) // 2
        valid = wanted & (k >= 0) & (k < offsets) & (row >= 0) & (row < total_pairs)
        weight = coupling_ref[jnp.clip(row, 0, total_pairs - 1), jnp.clip(k, 0, offsets - 1)]
        weight = jnp.where(valid, weight, 0.0)
        term = weight * amp_ref[j].astype(jnp.float32)
        total = term if total is None else total + term
    for more in refs[:-1]:
        total = total + more[...].astype(jnp.float32)
    refs[-1][...] = total.astype(jnp.bfloat16)


def share(coupling, target_of, i, amplitudes, arrived):
    pairs, rows, width = amplitudes.shape
    step = min(rows, 64)
    flat = pl.BlockSpec((step, width), lambda r: (r, 0))
    return pl.pallas_call(
        functools.partial(share_kernel, target_of, i),
        grid=(rows // step,),
        in_specs=[
            pl.BlockSpec(memory_space=pltpu.SMEM),
            pl.BlockSpec((pairs, step, width), lambda r: (0, r, 0)),
        ]
        + [flat] * len(arrived),
        out_specs=flat,
        out_shape=jax.ShapeDtypeStruct((rows, width), jnp.bfloat16),
        compiler_params=pltpu.CompilerParams(vmem_limit_bytes=VMEM_BYTES),
        cost_estimate=pl.CostEstimate(
            flops=2 * pairs * rows * width,
            bytes_accessed=2 * (pairs + 1 + len(arrived)) * rows * width,
            transcendentals=0,
        ),
        name="share",
    )(coupling, amplitudes, *arrived)


def cycle_kernel(mixed_ref, int_ref, out_ref):
    out_ref[0] = jnp.dot(
        mixed_ref[...], int_ref[...], preferred_element_type=jnp.float32
    ).astype(jnp.bfloat16)


def cycle_of(mixed, integrals, count):
    rows, width = mixed.shape
    part = width // count
    return pl.pallas_call(
        cycle_kernel,
        grid=(count,),
        in_specs=[
            pl.BlockSpec((rows, width), lambda n: (0, 0)),
            pl.BlockSpec((width, part), lambda n: (0, n)),
        ],
        out_specs=pl.BlockSpec((1, rows, part), lambda n: (n, 0, 0)),
        out_shape=jax.ShapeDtypeStruct((count, rows, part), jnp.bfloat16),
        compiler_params=pltpu.CompilerParams(vmem_limit_bytes=VMEM_BYTES),
        cost_estimate=pl.CostEstimate(
            flops=2 * rows * width * width,
            bytes_accessed=2 * (width * width + 2 * rows * width),
            transcendentals=0,
        ),
        name="cycle",
    )(mixed, integrals)


def update_kernel(slot, pair_ref, cyc_ref, swap_ref, erow_ref, ecol_ref, lrow_ref, mcol_ref, *refs):
    out_ref = refs[-1]
    rows, part = cyc_ref.shape[1], cyc_ref.shape[2]
    swapped = swap_ref[0].astype(jnp.float32).T
    residual = cyc_ref[0].astype(jnp.float32) + swapped
    denom = erow_ref[...] + ecol_ref[...] - pair_ref[0]
    ratio = residual / denom * lrow_ref[...]
    for t in range(rows // slot):
        out_ref[0, t * slot : (t + 1) * slot, :] = (
            ratio[t * slot : (t + 1) * slot, :] * mcol_ref[t : t + 1, :]
        ).astype(jnp.bfloat16)


def update_of(index, pairs, slot, pair, cycle, swapped, erow, ecol, lrow, mcol, before):
    count, rows, part = cycle.shape
    width = count * part
    tiles = mcol.shape[0]
    block = pl.BlockSpec((1, rows, part), lambda n: (n, 0, 0))
    column = pl.BlockSpec((rows, 1), lambda n: (0, 0))
    extra = [] if before is None else [before]
    return pl.pallas_call(
        functools.partial(update_kernel, slot),
        grid=(count,),
        in_specs=[
            pl.BlockSpec(memory_space=pltpu.SMEM),
            block,
            block,
            column,
            pl.BlockSpec((1, part), lambda n: (0, n)),
            column,
            pl.BlockSpec((tiles, part), lambda n: (0, n)),
        ]
        + [pl.BlockSpec(memory_space=pl.ANY)] * len(extra),
        out_specs=pl.BlockSpec((1, rows, part), lambda n: (index, 0, n)),
        out_shape=jax.ShapeDtypeStruct((pairs, rows, width), jnp.bfloat16),
        input_output_aliases={7: 0} if extra else {},
        compiler_params=pltpu.CompilerParams(vmem_limit_bytes=VMEM_BYTES),
        cost_estimate=pl.CostEstimate(
            flops=10 * rows * width, bytes_accessed=6 * rows * width, transcendentals=0
        ),
        name="update",
    )(pair, cycle, swapped, erow, ecol, lrow, mcol, *extra)


def to_self(w):
    return w, w >= 0


def to_next(w):
    return w + 1, w >= 0


def to_last(w):
    return w - 1, w >= 0


def to_partner(w):
    return jnp.where(lax.rem(w, 2) == 0, w + 1, w - 1), w >= 0


def to_opposite(w):
    return 3 - w, (w == 1) | (w == 2)


def after(value, earlier):
    return value if earlier is None else lax.optimization_barrier((value, earlier))[0]


def per_device(amplitudes, integrals, coupling, pair_energy, virtual_energy, tile_sizes, blocks):
    pairs, rows, width = amplitudes.shape
    wide, count = lax.axis_size("wide"), lax.axis_size("perm")
    m = lax.axis_index("perm")
    full = lax.all_gather(integrals, "perm", axis=0, tiled=True)

    square = wide == 4
    if square:
        relay_to = [(1, 3), (2, 0)]
        across_to = [(0, 1), (1, 0), (2, 3), (3, 2)]
    else:
        up = [(s, s + 1) for s in range(wide - 1)]
        down = [(s + 1, s) for s in range(wide - 1)]

    tiles = tile_sizes.shape[0]
    slot = width // tiles
    live = (jnp.arange(slot)[None, :] < tile_sizes[:, None]).reshape(width).astype(jnp.float32)
    start = m * rows
    lrow = lax.dynamic_slice_in_dim(live, start, rows, 0)[:, None]
    erow = lax.dynamic_slice_in_dim(virtual_energy, start, rows, 0)[:, None]
    ecol = virtual_energy[None, :]
    here = lax.dynamic_slice_in_dim(blocks, start // slot, rows // slot, 1).astype(jnp.float32)
    mcol = jnp.repeat(here, slot, axis=2) * live[None, None, :]

    first = second = None
    mixed = []
    for i in range(pairs):
        if square:
            term = after(share(coupling, to_opposite, i, amplitudes, []), first)
            first = lax.ppermute(term, "wide", relay_to)
            term = after(share(coupling, to_partner, i, amplitudes, [first]), second)
            second = lax.ppermute(term, "wide", across_to)
            arrived = [second]
        else:
            term = after(share(coupling, to_next, i, amplitudes, []), first)
            first = lax.ppermute(term, "wide", up)
            term = after(share(coupling, to_last, i, amplitudes, []), second)
            second = lax.ppermute(term, "wide", down)
            arrived = [first, second]
        mixed.append(share(coupling, to_self, i, amplitudes, arrived))
    result = None
    swapped = None
    for i in range(pairs):
        cycle = cycle_of(mixed[i], full, count)
        swapped = lax.all_to_all(after(cycle, swapped), "perm", split_axis=0, concat_axis=0)
        result = update_of(
            i, pairs, slot, pair_energy[i : i + 1], cycle, swapped, erow, ecol, lrow, mcol[i], result
        )
    return result


def solution(mesh):
    in_specs = (
        P("wide", "perm", None),
        P("perm", None),
        P(),
        P("wide"),
        P(),
        P(),
        P("wide", None, None),
    )
    out_specs = P("wide", "perm", None)
    return jax.shard_map(
        per_device, mesh=mesh, in_specs=in_specs, out_specs=out_specs, check_vma=False
    )
```

```python
import functools

import jax
import jax.numpy as jnp
from jax import lax
from jax.experimental import pallas as pl
from jax.experimental.pallas import tpu as pltpu
from jax.sharding import PartitionSpec as P

VMEM_BYTES = 48 * 1024 * 1024


def share_kernel(target_of, i, coupling_ref, amp_ref, *refs):
    pairs = amp_ref.shape[0]
    total_pairs, offsets = coupling_ref.shape
    source = lax.axis_index("wide")
    target, wanted = target_of(source)
    row = target * pairs + i
    total = None
    for j in range(pairs):
        k = (source - target) * pairs + j - i + (offsets - 1) // 2
        valid = wanted & (k >= 0) & (k < offsets) & (row >= 0) & (row < total_pairs)
        weight = coupling_ref[jnp.clip(row, 0, total_pairs - 1), jnp.clip(k, 0, offsets - 1)]
        weight = jnp.where(valid, weight, 0.0)
        term = weight * amp_ref[j].astype(jnp.float32)
        total = term if total is None else total + term
    for more in refs[:-1]:
        total = total + more[...].astype(jnp.float32)
    refs[-1][...] = total.astype(jnp.bfloat16)


def share(coupling, target_of, i, amplitudes, arrived):
    pairs, rows, width = amplitudes.shape
    step = min(rows, 64)
    flat = pl.BlockSpec((step, width), lambda r: (r, 0))
    return pl.pallas_call(
        functools.partial(share_kernel, target_of, i),
        grid=(rows // step,),
        in_specs=[
            pl.BlockSpec(memory_space=pltpu.SMEM),
            pl.BlockSpec((pairs, step, width), lambda r: (0, r, 0)),
        ]
        + [flat] * len(arrived),
        out_specs=flat,
        out_shape=jax.ShapeDtypeStruct((rows, width), jnp.bfloat16),
        compiler_params=pltpu.CompilerParams(vmem_limit_bytes=VMEM_BYTES),
        cost_estimate=pl.CostEstimate(
            flops=2 * pairs * rows * width,
            bytes_accessed=2 * (pairs + 1 + len(arrived)) * rows * width,
            transcendentals=0,
        ),
        name="share",
    )(coupling, amplitudes, *arrived)


def cycle_kernel(mixed_ref, int_ref, out_ref):
    out_ref[0] = jnp.dot(
        mixed_ref[...], int_ref[...], preferred_element_type=jnp.float32
    ).astype(jnp.bfloat16)


def cycle_of(mixed, integrals, count):
    rows, width = mixed.shape
    part = width // count
    return pl.pallas_call(
        cycle_kernel,
        grid=(count,),
        in_specs=[
            pl.BlockSpec((rows, width), lambda n: (0, 0)),
            pl.BlockSpec((width, part), lambda n: (0, n)),
        ],
        out_specs=pl.BlockSpec((1, rows, part), lambda n: (n, 0, 0)),
        out_shape=jax.ShapeDtypeStruct((count, rows, part), jnp.bfloat16),
        compiler_params=pltpu.CompilerParams(vmem_limit_bytes=VMEM_BYTES),
        cost_estimate=pl.CostEstimate(
            flops=2 * rows * width * width,
            bytes_accessed=2 * (width * width + 2 * rows * width),
            transcendentals=0,
        ),
        name="cycle",
    )(mixed, integrals)


def update_kernel(slot, pair_ref, cyc_ref, swap_ref, erow_ref, ecol_ref, lrow_ref, mcol_ref, *refs):
    out_ref = refs[-1]
    rows, part = cyc_ref.shape[1], cyc_ref.shape[2]
    swapped = swap_ref[0].astype(jnp.float32).T
    residual = cyc_ref[0].astype(jnp.float32) + swapped
    denom = erow_ref[...] + ecol_ref[...] - pair_ref[0]
    ratio = residual / denom * lrow_ref[...]
    for t in range(rows // slot):
        out_ref[0, t * slot : (t + 1) * slot, :] = (
            ratio[t * slot : (t + 1) * slot, :] * mcol_ref[t : t + 1, :]
        ).astype(jnp.bfloat16)


def update_of(index, pairs, slot, pair, cycle, swapped, erow, ecol, lrow, mcol, before):
    count, rows, part = cycle.shape
    width = count * part
    tiles = mcol.shape[0]
    block = pl.BlockSpec((1, rows, part), lambda n: (n, 0, 0))
    column = pl.BlockSpec((rows, 1), lambda n: (0, 0))
    extra = [] if before is None else [before]
    return pl.pallas_call(
        functools.partial(update_kernel, slot),
        grid=(count,),
        in_specs=[
            pl.BlockSpec(memory_space=pltpu.SMEM),
            block,
            block,
            column,
            pl.BlockSpec((1, part), lambda n: (0, n)),
            column,
            pl.BlockSpec((tiles, part), lambda n: (0, n)),
        ]
        + [pl.BlockSpec(memory_space=pl.ANY)] * len(extra),
        out_specs=pl.BlockSpec((1, rows, part), lambda n: (index, 0, n)),
        out_shape=jax.ShapeDtypeStruct((pairs, rows, width), jnp.bfloat16),
        input_output_aliases={7: 0} if extra else {},
        compiler_params=pltpu.CompilerParams(vmem_limit_bytes=VMEM_BYTES),
        cost_estimate=pl.CostEstimate(
            flops=10 * rows * width, bytes_accessed=6 * rows * width, transcendentals=0
        ),
        name="update",
    )(pair, cycle, swapped, erow, ecol, lrow, mcol, *extra)


MESH = pl.DeviceIdType.MESH
STRIP = 16


def square_kernel(slot, coupling_ref, pair_ref, amp_ref, int_ref, erow_ref, ecol_ref, lrow_ref, mcol_ref,
                  out_ref, held, passed, relayed, sent, landed, mixed, cyc, swap, done,
                  own_sem, right_send, right_recv, left_send, left_recv, core_send, core_recv,
                  pass_send, pass_recv, side_send, side_recv, turn_send, turn_recv, keep_sem, out_sem):
    pairs, rows, width = amp_ref.shape
    total_pairs, offsets = coupling_ref.shape
    count = width // rows
    chips = count // 2
    w, m = lax.axis_index("wide"), lax.axis_index("perm")
    z, c = m // 2, lax.rem(m, 2)
    twin = m + 1 - 2 * c
    beside = w + 1 - 2 * lax.rem(w, 2)
    above = lax.rem(w + 2, 4)
    inner = (w == 1) | (w == 2)
    outer = (w == 0) | (w == 3)

    barrier = pltpu.get_barrier_semaphore()
    for k in range(1, count):
        pl.semaphore_signal(barrier, inc=1, device_id={"perm": lax.rem(m + k, count)}, device_id_type=MESH)
    for other in (beside, above):
        pl.semaphore_signal(barrier, inc=1, device_id={"wide": other}, device_id_type=MESH)
    pl.semaphore_wait(barrier, count + 1)

    def block(index):
        return held.at[pl.ds(pl.multiple_of(index * rows, rows), rows)]

    def move(src, dst, send, recv, where):
        return pltpu.make_async_remote_copy(
            src_ref=src, dst_ref=dst, send_sem=send, recv_sem=recv, device_id=where, device_id_type=MESH
        )

    def right(b, t):
        return move(block(b * 2 + c), block(b * 2 + c), right_send.at[t], right_recv.at[t], {"perm": m + 2})

    def left(b, t):
        return move(block(b * 2 + c), block(b * 2 + c), left_send.at[t], left_recv.at[t], {"perm": m - 2})

    def across(b, core, u):
        return move(block(b * 2 + core), block(b * 2 + core), core_send.at[u], core_recv.at[u], {"perm": twin})

    def relay(i):
        return move(passed.at[i], relayed.at[i], pass_send.at[i], pass_recv.at[i], {"wide": above})

    def side(i):
        return move(sent.at[i], landed.at[i], side_send.at[i], side_recv.at[i], {"wide": beside})

    def turn(i, s, source):
        return move(cyc.at[i, s], swap.at[i, source], turn_send.at[i, s], turn_recv.at[i, source], {"perm": s})

    def spread(t):
        @pl.when((z - t >= 0) & (z + 1 < chips))
        def _():
            right(z - t, t).start()

        @pl.when((z + t < chips) & (z >= 1))
        def _():
            left(z + t, t).start()

    def gather_step(t):
        @pl.when(z - 1 - t >= 0)
        def _():
            right(z - 1 - t, t).wait_recv()

        @pl.when(z + 1 + t < chips)
        def _():
            left(z + 1 + t, t).wait_recv()

        if t + 1 < chips - 1:
            spread(t + 1)

        @pl.when(z - 1 - t >= 0)
        def _():
            across(z - 1 - t, c, 1 + t).start()

        @pl.when(z + 1 + t < chips)
        def _():
            across(z + 1 + t, c, chips + t).start()

    def gather_end():
        across(z, 1 - c, 0).wait_recv()
        for t in range(chips - 1):
            @pl.when(z - 1 - t >= 0)
            def _():
                across(z - 1 - t, 1 - c, 1 + t).wait_recv()

            @pl.when(z + 1 + t < chips)
            def _():
                across(z + 1 + t, 1 - c, chips + t).wait_recv()

    def add_up(target, i, dst, extra):
        row = target * pairs + i
        weights = []
        for j in range(pairs):
            k = (w - target) * pairs + j - i + (offsets - 1) // 2
            valid = (k >= 0) & (k < offsets)
            weights.append(jnp.where(valid, coupling_ref[row, jnp.clip(k, 0, offsets - 1)], 0.0))

        @pl.loop(0, rows // STRIP)
        def _(r):
            strip = pl.ds(pl.multiple_of(r * STRIP, STRIP), STRIP)
            total = weights[0] * amp_ref[0, strip, :].astype(jnp.float32)
            for j in range(1, pairs):
                total = total + weights[j] * amp_ref[j, strip, :].astype(jnp.float32)
            if extra is not None:
                total = total + extra[i, strip, :].astype(jnp.float32)
            dst[i, strip, :] = total.astype(jnp.bfloat16)

    def side_step(i):
        @pl.when(inner)
        def _():
            add_up(beside, i, sent, None)

        @pl.when(outer)
        def _():
            relay(i).wait_recv()
            add_up(beside, i, sent, relayed)

        if i > 0:
            side(i - 1).wait_send()
        side(i).start()

    def relay_step(i):
        @pl.when(inner)
        def _():
            if i > 0:
                relay(i - 1).wait_send()
            relay(i).start()

    def mix_step(i):
        side(i).wait_recv()
        add_up(w, i, mixed, landed)

    def cycle_step(i):
        @pl.loop(1, count + 1)
        def _(k):
            s = lax.rem(m + k, count)
            columns = pl.ds(pl.multiple_of(s * rows, rows), rows)
            cyc[i, s] = jnp.dot(
                mixed[i], held[:, columns], preferred_element_type=jnp.float32
            ).astype(jnp.bfloat16)

            @pl.when(s != m)
            def _():
                turn(i, s, m).start()

        pltpu.make_async_copy(cyc.at[i, m], swap.at[i, m], keep_sem.at[i]).start()

    def update_step(i):
        pltpu.make_async_copy(cyc.at[i, m], swap.at[i, m], keep_sem.at[i]).wait()
        for k in range(1, count):
            s = lax.rem(m + k, count)
            turn(i, s, s).wait_recv()

        @pl.loop(0, count)
        def _(s):
            columns = pl.ds(pl.multiple_of(s * rows, rows), rows)
            residual = cyc[i, s].astype(jnp.float32) + swap[i, s].astype(jnp.float32).T
            denom = erow_ref[...] + ecol_ref[:, columns] - pair_ref[i]
            ratio = residual / denom * lrow_ref[...]
            for t in range(rows // slot):
                done[i, t * slot : (t + 1) * slot, columns] = (
                    ratio[t * slot : (t + 1) * slot, :] * mcol_ref[i, t : t + 1, columns]
                ).astype(jnp.bfloat16)

        pltpu.make_async_copy(done.at[i], out_ref.at[i], out_sem.at[i]).start()

    keep = pltpu.make_async_copy(int_ref, block(m), own_sem)
    keep.start()
    keep.wait()
    spread(0)
    across(z, c, 0).start()
    for i in range(pairs):
        @pl.when(inner)
        def _():
            add_up(3 - w, i, passed, None)

        if i == 0:
            relay_step(0)

    ready = 0
    for i in range(max(pairs, chips - 1) + 1):
        if i < pairs:
            side_step(i)
        if i + 1 < pairs:
            relay_step(i + 1)
        if i < chips - 1:
            gather_step(i)
        if 1 <= i <= pairs:
            mix_step(i - 1)
        if i == chips - 2:
            gather_end()
        if i >= chips - 2:
            while ready < min(i, pairs):
                cycle_step(ready)
                ready += 1
    for i in range(pairs):
        update_step(i)

    across(z, c, 0).wait_send()
    for t in range(chips - 1):
        @pl.when((z - t >= 0) & (z + 1 < chips))
        def _():
            right(z - t, t).wait_send()

        @pl.when((z + t < chips) & (z >= 1))
        def _():
            left(z + t, t).wait_send()

        @pl.when(z - 1 - t >= 0)
        def _():
            across(z - 1 - t, c, 1 + t).wait_send()

        @pl.when(z + 1 + t < chips)
        def _():
            across(z + 1 + t, c, chips + t).wait_send()

    @pl.when(inner)
    def _():
        relay(pairs - 1).wait_send()

    side(pairs - 1).wait_send()
    for i in range(pairs):
        for k in range(1, count):
            turn(i, lax.rem(m + k, count), m).wait_send()
        pltpu.make_async_copy(done.at[i], out_ref.at[i], out_sem.at[i]).wait()


def square_call(slot, coupling, pair_energy, amplitudes, integrals, erow, ecol, lrow, mcol):
    pairs, rows, width = amplitudes.shape
    count = width // rows
    chips = count // 2
    smem = pl.BlockSpec(memory_space=pltpu.SMEM)
    vmem = pl.BlockSpec(memory_space=pltpu.VMEM)
    anywhere = pl.BlockSpec(memory_space=pl.ANY)
    dma = pltpu.SemaphoreType.DMA
    matrices = pltpu.VMEM((pairs, rows, width), jnp.bfloat16)
    squares = pltpu.VMEM((pairs, count, rows, rows), jnp.bfloat16)
    return pl.pallas_call(
        functools.partial(square_kernel, slot),
        in_specs=[smem, smem, vmem, anywhere, vmem, vmem, vmem, vmem],
        out_specs=anywhere,
        out_shape=jax.ShapeDtypeStruct((pairs, rows, width), jnp.bfloat16),
        scratch_shapes=[
            pltpu.VMEM((width, width), jnp.bfloat16),
            matrices, matrices, matrices, matrices, matrices,
            squares, squares,
            matrices,
            dma,
            dma((chips - 1,)), dma((chips - 1,)), dma((chips - 1,)), dma((chips - 1,)),
            dma((2 * chips - 1,)), dma((2 * chips - 1,)),
            dma((pairs,)), dma((pairs,)), dma((pairs,)), dma((pairs,)),
            dma((pairs, count)), dma((pairs, count)),
            dma((pairs,)), dma((pairs,)),
        ],
        compiler_params=pltpu.CompilerParams(
            collective_id=0, has_side_effects=True, vmem_limit_bytes=56 * 1024 * 1024
        ),
        name="square",
    )(coupling, pair_energy, amplitudes, integrals, erow, ecol, lrow, mcol)


def to_self(w):
    return w, w >= 0


def to_next(w):
    return w + 1, w >= 0


def to_last(w):
    return w - 1, w >= 0


def after(value, earlier):
    return value if earlier is None else lax.optimization_barrier((value, earlier))[0]


def per_device(amplitudes, integrals, coupling, pair_energy, virtual_energy, tile_sizes, blocks):
    pairs, rows, width = amplitudes.shape
    wide, count = lax.axis_size("wide"), lax.axis_size("perm")
    m = lax.axis_index("perm")

    tiles = tile_sizes.shape[0]
    slot = width // tiles
    live = (jnp.arange(slot)[None, :] < tile_sizes[:, None]).reshape(width).astype(jnp.float32)
    start = m * rows
    lrow = lax.dynamic_slice_in_dim(live, start, rows, 0)[:, None]
    erow = lax.dynamic_slice_in_dim(virtual_energy, start, rows, 0)[:, None]
    ecol = virtual_energy[None, :]
    here = lax.dynamic_slice_in_dim(blocks, start // slot, rows // slot, 1).astype(jnp.float32)
    mcol = jnp.repeat(here, slot, axis=2) * live[None, None, :]

    if wide == 4 and count % 2 == 0 and count * rows == width:
        return square_call(slot, coupling, pair_energy, amplitudes, integrals, erow, ecol, lrow, mcol)

    full = lax.all_gather(integrals, "perm", axis=0, tiled=True)
    up = [(s, s + 1) for s in range(wide - 1)]
    down = [(s + 1, s) for s in range(wide - 1)]
    first = second = None
    mixed = []
    for i in range(pairs):
        term = after(share(coupling, to_next, i, amplitudes, []), first)
        first = lax.ppermute(term, "wide", up)
        term = after(share(coupling, to_last, i, amplitudes, []), second)
        second = lax.ppermute(term, "wide", down)
        arrived = [first, second]
        mixed.append(share(coupling, to_self, i, amplitudes, arrived))
    result = None
    swapped = None
    for i in range(pairs):
        cycle = cycle_of(mixed[i], full, count)
        swapped = lax.all_to_all(after(cycle, swapped), "perm", split_axis=0, concat_axis=0)
        result = update_of(
            i, pairs, slot, pair_energy[i : i + 1], cycle, swapped, erow, ecol, lrow, mcol[i], result
        )
    return result


def solution(mesh):
    in_specs = (
        P("wide", "perm", None),
        P("perm", None),
        P(),
        P("wide"),
        P(),
        P(),
        P("wide", None, None),
    )
    out_specs = P("wide", "perm", None)
    return jax.shard_map(
        per_device, mesh=mesh, in_specs=in_specs, out_specs=out_specs, check_vma=False
    )
```

```python
import functools

import jax
import jax.numpy as jnp
from jax import lax
from jax.experimental import pallas as pl
from jax.experimental.pallas import tpu as pltpu
from jax.sharding import PartitionSpec as P

VMEM_BYTES = 48 * 1024 * 1024


def share_kernel(target_of, i, coupling_ref, amp_ref, *refs):
    pairs = amp_ref.shape[0]
    total_pairs, offsets = coupling_ref.shape
    source = lax.axis_index("wide")
    target, wanted = target_of(source)
    row = target * pairs + i
    total = None
    for j in range(pairs):
        k = (source - target) * pairs + j - i + (offsets - 1) // 2
        valid = wanted & (k >= 0) & (k < offsets) & (row >= 0) & (row < total_pairs)
        weight = coupling_ref[jnp.clip(row, 0, total_pairs - 1), jnp.clip(k, 0, offsets - 1)]
        weight = jnp.where(valid, weight, 0.0)
        term = weight * amp_ref[j].astype(jnp.float32)
        total = term if total is None else total + term
    for more in refs[:-1]:
        total = total + more[...].astype(jnp.float32)
    refs[-1][...] = total.astype(jnp.bfloat16)


def share(coupling, target_of, i, amplitudes, arrived):
    pairs, rows, width = amplitudes.shape
    step = min(rows, 64)
    flat = pl.BlockSpec((step, width), lambda r: (r, 0))
    return pl.pallas_call(
        functools.partial(share_kernel, target_of, i),
        grid=(rows // step,),
        in_specs=[
            pl.BlockSpec(memory_space=pltpu.SMEM),
            pl.BlockSpec((pairs, step, width), lambda r: (0, r, 0)),
        ]
        + [flat] * len(arrived),
        out_specs=flat,
        out_shape=jax.ShapeDtypeStruct((rows, width), jnp.bfloat16),
        compiler_params=pltpu.CompilerParams(vmem_limit_bytes=VMEM_BYTES),
        cost_estimate=pl.CostEstimate(
            flops=2 * pairs * rows * width,
            bytes_accessed=2 * (pairs + 1 + len(arrived)) * rows * width,
            transcendentals=0,
        ),
        name="share",
    )(coupling, amplitudes, *arrived)


def cycle_kernel(mixed_ref, int_ref, out_ref):
    out_ref[0] = jnp.dot(
        mixed_ref[...], int_ref[...], preferred_element_type=jnp.float32
    ).astype(jnp.bfloat16)


def cycle_of(mixed, integrals, count):
    rows, width = mixed.shape
    part = width // count
    return pl.pallas_call(
        cycle_kernel,
        grid=(count,),
        in_specs=[
            pl.BlockSpec((rows, width), lambda n: (0, 0)),
            pl.BlockSpec((width, part), lambda n: (0, n)),
        ],
        out_specs=pl.BlockSpec((1, rows, part), lambda n: (n, 0, 0)),
        out_shape=jax.ShapeDtypeStruct((count, rows, part), jnp.bfloat16),
        compiler_params=pltpu.CompilerParams(vmem_limit_bytes=VMEM_BYTES),
        cost_estimate=pl.CostEstimate(
            flops=2 * rows * width * width,
            bytes_accessed=2 * (width * width + 2 * rows * width),
            transcendentals=0,
        ),
        name="cycle",
    )(mixed, integrals)


def update_kernel(slot, pair_ref, cyc_ref, swap_ref, erow_ref, ecol_ref, lrow_ref, mcol_ref, *refs):
    out_ref = refs[-1]
    rows, part = cyc_ref.shape[1], cyc_ref.shape[2]
    swapped = swap_ref[0].astype(jnp.float32).T
    residual = cyc_ref[0].astype(jnp.float32) + swapped
    denom = erow_ref[...] + ecol_ref[...] - pair_ref[0]
    ratio = residual / denom * lrow_ref[...]
    for t in range(rows // slot):
        out_ref[0, t * slot : (t + 1) * slot, :] = (
            ratio[t * slot : (t + 1) * slot, :] * mcol_ref[t : t + 1, :]
        ).astype(jnp.bfloat16)


def update_of(index, pairs, slot, pair, cycle, swapped, erow, ecol, lrow, mcol, before):
    count, rows, part = cycle.shape
    width = count * part
    tiles = mcol.shape[0]
    block = pl.BlockSpec((1, rows, part), lambda n: (n, 0, 0))
    column = pl.BlockSpec((rows, 1), lambda n: (0, 0))
    extra = [] if before is None else [before]
    return pl.pallas_call(
        functools.partial(update_kernel, slot),
        grid=(count,),
        in_specs=[
            pl.BlockSpec(memory_space=pltpu.SMEM),
            block,
            block,
            column,
            pl.BlockSpec((1, part), lambda n: (0, n)),
            column,
            pl.BlockSpec((tiles, part), lambda n: (0, n)),
        ]
        + [pl.BlockSpec(memory_space=pl.ANY)] * len(extra),
        out_specs=pl.BlockSpec((1, rows, part), lambda n: (index, 0, n)),
        out_shape=jax.ShapeDtypeStruct((pairs, rows, width), jnp.bfloat16),
        input_output_aliases={7: 0} if extra else {},
        compiler_params=pltpu.CompilerParams(vmem_limit_bytes=VMEM_BYTES),
        cost_estimate=pl.CostEstimate(
            flops=10 * rows * width, bytes_accessed=6 * rows * width, transcendentals=0
        ),
        name="update",
    )(pair, cycle, swapped, erow, ecol, lrow, mcol, *extra)


MESH = pl.DeviceIdType.MESH
STRIP = 16


def square_kernel(slot, coupling_ref, pair_ref, size_ref, blocks_ref, amp_ref, int_ref, energy_ref,
                  out_ref, held, passed, relayed, sent, landed, mixed, cyc, swap, erow,
                  own_sem, right_send, right_recv, left_send, left_recv, core_send, core_recv, piece_send, piece_recv, core2_send, core2_recv,
                  pass_send, pass_recv, side_send, side_recv, turn_send, turn_recv, keep_sem):
    pairs, rows, width = amp_ref.shape
    total_pairs, offsets = coupling_ref.shape
    count = width // rows
    chips = count // 2
    w, m = lax.axis_index("wide"), lax.axis_index("perm")
    z, c = m // 2, lax.rem(m, 2)
    twin = m + 1 - 2 * c
    beside = w + 1 - 2 * lax.rem(w, 2)
    above = lax.rem(w + 2, 4)
    inner = (w == 1) | (w == 2)
    outer = (w == 0) | (w == 3)
    edge = rows // STRIP * 5 // 16 * STRIP
    most = rows - edge
    z_from = jnp.where(inner, edge, 0)
    give_from = jnp.where(inner, most, 0)
    lack_from = jnp.where(inner, 0, most)
    friend = jnp.where(inner, beside, above)
    lasts = chips - 1

    barrier = pltpu.get_barrier_semaphore()
    for k in range(1, count):
        pl.semaphore_signal(barrier, inc=1, device_id={"perm": lax.rem(m + k, count)}, device_id_type=MESH)
    for other in (beside, above):
        pl.semaphore_signal(barrier, inc=1, device_id={"wide": other}, device_id_type=MESH)
    pl.semaphore_wait(barrier, count + 1)

    def block(index):
        return held.at[pl.ds(pl.multiple_of(index * rows, rows), rows)]

    def move(src, dst, send, recv, where):
        return pltpu.make_async_remote_copy(
            src_ref=src, dst_ref=dst, send_sem=send, recv_sem=recv, device_id=where, device_id_type=MESH
        )

    def part(index, start, size):
        return held.at[pl.ds(pl.multiple_of(index * rows + start, STRIP), size)]

    def right(b, t):
        here = part(b * 2 + c, z_from, most)
        return move(here, here, right_send.at[t], right_recv.at[t], {"perm": m + 2})

    def left(b, t):
        here = part(b * 2 + c, z_from, most)
        return move(here, here, left_send.at[t], left_recv.at[t], {"perm": m - 2})

    def own_across(core):
        here = block(z * 2 + core)
        return move(here, here, core_send.at[0], core_recv.at[0], {"perm": twin})

    def across(b, core, u):
        here = part(b * 2 + core, z_from, most)
        return move(here, here, core_send.at[1 + u], core_recv.at[1 + u], {"perm": twin})

    def piece(b, start, u):
        here = part(b * 2 + c, start, edge)
        return move(here, here, piece_send.at[u], piece_recv.at[u], {"wide": friend})

    def piece_across(b, core, u):
        here = part(b * 2 + core, lack_from, edge)
        return move(here, here, core2_send.at[u], core2_recv.at[u], {"perm": twin})

    def arrivals(t, action):
        @pl.when(z - 1 - t >= 0)
        def _():
            action(z - 1 - t, t)

        @pl.when(z + 1 + t < chips)
        def _():
            action(z + 1 + t, lasts + t)

    def relay(i):
        return move(passed.at[i], relayed.at[i], pass_send.at[i], pass_recv.at[i], {"wide": above})

    def side(i):
        return move(sent.at[i], landed.at[i], side_send.at[i], side_recv.at[i], {"wide": beside})

    def turn(i, s, source):
        return move(cyc.at[i, s], swap.at[i, source], turn_send.at[i, s], turn_recv.at[i, source], {"perm": s})

    def spread(t):
        @pl.when((z - t >= 0) & (z + 1 < chips))
        def _():
            right(z - t, t).start()

        @pl.when((z + t < chips) & (z >= 1))
        def _():
            left(z + t, t).start()

    def gather_step(t):
        @pl.when(z - 1 - t >= 0)
        def _():
            right(z - 1 - t, t).wait_recv()

        @pl.when(z + 1 + t < chips)
        def _():
            left(z + 1 + t, t).wait_recv()

        if t + 1 < lasts:
            spread(t + 1)

        def pass_on(b, u):
            piece(b, give_from, u).start()
            across(b, c, u).start()

        arrivals(t, pass_on)

    def piece_step(t):
        def pass_on(b, u):
            piece(b, lack_from, u).wait_recv()
            piece_across(b, c, u).start()

        arrivals(t, pass_on)

    def gather_end():
        own_across(1 - c).wait_recv()

        def finish(b, u):
            across(b, 1 - c, u).wait_recv()
            piece_across(b, 1 - c, u).wait_recv()

        for t in range(lasts):
            arrivals(t, finish)

    def add_up(target, i, dst, extra):
        row = target * pairs + i
        weights = []
        for j in range(pairs):
            k = (w - target) * pairs + j - i + (offsets - 1) // 2
            valid = (k >= 0) & (k < offsets)
            weights.append(jnp.where(valid, coupling_ref[row, jnp.clip(k, 0, offsets - 1)], 0.0))

        @pl.loop(0, rows // STRIP)
        def _(r):
            strip = pl.ds(pl.multiple_of(r * STRIP, STRIP), STRIP)
            total = weights[0] * amp_ref[0, strip, :].astype(jnp.float32)
            for j in range(1, pairs):
                total = total + weights[j] * amp_ref[j, strip, :].astype(jnp.float32)
            if extra is not None:
                total = total + extra[i, strip, :].astype(jnp.float32)
            dst[i, strip, :] = total.astype(jnp.bfloat16)

    def side_inner(i):
        @pl.when(inner)
        def _():
            add_up(beside, i, sent, None)
            side(i).start()

    def side_outer(i):
        @pl.when(outer)
        def _():
            relay(i).wait_recv()
            add_up(beside, i, sent, relayed)
            side(i).start()

    def relay_step(i):
        @pl.when(inner)
        def _():
            if i > 0:
                relay(i - 1).wait_send()
            relay(i).start()

    def mix_step(i):
        side(i).wait_recv()
        add_up(w, i, mixed, landed)

    def cycle_step(i):
        @pl.loop(1, count + 1)
        def _(k):
            s = lax.rem(m + k, count)
            columns = pl.ds(pl.multiple_of(s * rows, rows), rows)
            cyc[i, s] = jnp.dot(
                mixed[i], held[:, columns], preferred_element_type=jnp.float32
            ).astype(jnp.bfloat16)

            @pl.when(s != m)
            def _():
                turn(i, s, m).start()

        pltpu.make_async_copy(cyc.at[i, m], swap.at[i, m], keep_sem.at[i]).start()

    def update_step(i):
        pltpu.make_async_copy(cyc.at[i, m], swap.at[i, m], keep_sem.at[i]).wait()
        for k in range(1, count):
            s = lax.rem(m + k, count)
            turn(i, s, s).wait_recv()

        @pl.loop(0, count)
        def _(s):
            columns = pl.ds(pl.multiple_of(s * rows, rows), rows)
            residual = cyc[i, s].astype(jnp.float32) + swap[i, s].astype(jnp.float32).T
            denom = erow[...] + (energy_ref[:, columns] - pair_ref[i])
            ratio = residual / denom
            across_at = lax.broadcasted_iota(jnp.int32, (slot, slot), 1)
            down_at = lax.broadcasted_iota(jnp.int32, (slot, slot), 0)
            for t in range(rows // slot):
                for u in range(rows // slot):
                    row_tile = m * (rows // slot) + t
                    column_tile = s * (rows // slot) + u
                    wanted = blocks_ref[i, row_tile, column_tile].astype(jnp.float32)
                    live = (down_at < size_ref[row_tile]) & (across_at < size_ref[column_tile])
                    tile = ratio[t * slot : (t + 1) * slot, u * slot : (u + 1) * slot]
                    place = pl.ds(pl.multiple_of(s * rows + u * slot, slot), slot)
                    out_ref[i, t * slot : (t + 1) * slot, place] = jnp.where(
                        live, tile * wanted, 0.0
                    ).astype(jnp.bfloat16)

    keep = pltpu.make_async_copy(int_ref, block(m), own_sem)
    keep.start()
    keep.wait()
    spread(0)
    own_across(c).start()
    for i in range(pairs):
        @pl.when(inner)
        def _():
            add_up(3 - w, i, passed, None)

        if i == 0:
            relay_step(0)
            side_inner(0)
    mine = energy_ref[:, pl.ds(pl.multiple_of(m * rows, rows), rows)]
    erow[...] = jnp.broadcast_to(mine, (rows, rows)).T

    gathered = begun = 0
    for i in range(pairs):
        while gathered < min(lasts, (3 * i + 2) // 2):
            gather_step(gathered)
            if gathered > 0:
                piece_step(gathered - 1)
            gathered += 1
        if gathered == lasts and begun < i - 1:
            if begun == 0:
                piece_step(lasts - 1)
                gather_end()
            while begun < i - 1:
                mix_step(begun)
                cycle_step(begun)
                begun += 1
        side_outer(i)
        if i + 1 < pairs:
            side_inner(i + 1)
            relay_step(i + 1)
    while gathered < lasts:
        gather_step(gathered)
        if gathered > 0:
            piece_step(gathered - 1)
        gathered += 1
    if begun == 0:
        piece_step(lasts - 1)
        gather_end()
    while begun < pairs:
        mix_step(begun)
        cycle_step(begun)
        begun += 1
    for i in range(pairs):
        update_step(i)

    own_across(c).wait_send()

    def all_gone(b, u):
        piece(b, give_from, u).wait_send()
        across(b, c, u).wait_send()
        piece_across(b, c, u).wait_send()

    for t in range(lasts):
        @pl.when((z - t >= 0) & (z + 1 < chips))
        def _():
            right(z - t, t).wait_send()

        @pl.when((z + t < chips) & (z >= 1))
        def _():
            left(z + t, t).wait_send()

        arrivals(t, all_gone)

    @pl.when(inner)
    def _():
        relay(pairs - 1).wait_send()

    for i in range(pairs):
        side(i).wait_send()
        for k in range(1, count):
            turn(i, lax.rem(m + k, count), m).wait_send()


def square_call(slot, coupling, pair_energy, tile_sizes, blocks, amplitudes, integrals, energy):
    pairs, rows, width = amplitudes.shape
    count = width // rows
    chips = count // 2
    smem = pl.BlockSpec(memory_space=pltpu.SMEM)
    vmem = pl.BlockSpec(memory_space=pltpu.VMEM)
    anywhere = pl.BlockSpec(memory_space=pl.ANY)
    dma = pltpu.SemaphoreType.DMA
    matrices = pltpu.VMEM((pairs, rows, width), jnp.bfloat16)
    squares = pltpu.VMEM((pairs, count, rows, rows), jnp.bfloat16)
    return pl.pallas_call(
        functools.partial(square_kernel, slot),
        in_specs=[smem, smem, smem, smem, vmem, anywhere, vmem],
        out_specs=vmem,
        out_shape=jax.ShapeDtypeStruct((pairs, rows, width), jnp.bfloat16),
        scratch_shapes=[
            pltpu.VMEM((width, width), jnp.bfloat16),
            matrices, matrices, matrices, matrices, matrices,
            squares, squares,
            pltpu.VMEM((rows, rows), jnp.float32),
            dma,
            dma((chips - 1,)), dma((chips - 1,)), dma((chips - 1,)), dma((chips - 1,)),
            dma((2 * chips - 1,)), dma((2 * chips - 1,)),
            dma((2 * chips - 2,)), dma((2 * chips - 2,)), dma((2 * chips - 2,)), dma((2 * chips - 2,)),
            dma((pairs,)), dma((pairs,)), dma((pairs,)), dma((pairs,)),
            dma((pairs, count)), dma((pairs, count)),
            dma((pairs,)),
        ],
        compiler_params=pltpu.CompilerParams(
            collective_id=0, has_side_effects=True, vmem_limit_bytes=56 * 1024 * 1024
        ),
        name="square",
    )(coupling, pair_energy, tile_sizes, blocks, amplitudes, integrals, energy)


def to_self(w):
    return w, w >= 0


def to_next(w):
    return w + 1, w >= 0


def to_last(w):
    return w - 1, w >= 0


def after(value, earlier):
    return value if earlier is None else lax.optimization_barrier((value, earlier))[0]


def per_device(amplitudes, integrals, coupling, pair_energy, virtual_energy, tile_sizes, blocks):
    pairs, rows, width = amplitudes.shape
    wide, count = lax.axis_size("wide"), lax.axis_size("perm")
    m = lax.axis_index("perm")

    tiles = tile_sizes.shape[0]
    slot = width // tiles
    if wide == 4 and count % 2 == 0 and count * rows == width and rows % slot == 0:
        return square_call(
            slot, coupling, pair_energy, tile_sizes, blocks, amplitudes, integrals, virtual_energy[None, :]
        )

    live = (jnp.arange(slot)[None, :] < tile_sizes[:, None]).reshape(width).astype(jnp.float32)
    start = m * rows
    lrow = lax.dynamic_slice_in_dim(live, start, rows, 0)[:, None]
    erow = lax.dynamic_slice_in_dim(virtual_energy, start, rows, 0)[:, None]
    ecol = virtual_energy[None, :]
    here = lax.dynamic_slice_in_dim(blocks, start // slot, rows // slot, 1).astype(jnp.float32)
    mcol = jnp.repeat(here, slot, axis=2) * live[None, None, :]

    full = lax.all_gather(integrals, "perm", axis=0, tiled=True)
    up = [(s, s + 1) for s in range(wide - 1)]
    down = [(s + 1, s) for s in range(wide - 1)]
    first = second = None
    mixed = []
    for i in range(pairs):
        term = after(share(coupling, to_next, i, amplitudes, []), first)
        first = lax.ppermute(term, "wide", up)
        term = after(share(coupling, to_last, i, amplitudes, []), second)
        second = lax.ppermute(term, "wide", down)
        arrived = [first, second]
        mixed.append(share(coupling, to_self, i, amplitudes, arrived))
    result = None
    swapped = None
    for i in range(pairs):
        cycle = cycle_of(mixed[i], full, count)
        swapped = lax.all_to_all(after(cycle, swapped), "perm", split_axis=0, concat_axis=0)
        result = update_of(
            i, pairs, slot, pair_energy[i : i + 1], cycle, swapped, erow, ecol, lrow, mcol[i], result
        )
    return result


def solution(mesh):
    in_specs = (
        P("wide", "perm", None),
        P("perm", None),
        P(),
        P("wide"),
        P(),
        P(),
        P("wide", None, None),
    )
    out_specs = P("wide", "perm", None)
    return jax.shard_map(
        per_device, mesh=mesh, in_specs=in_specs, out_specs=out_specs, check_vma=False
    )
```

```python
import functools

import jax
import jax.numpy as jnp
from jax import lax
from jax.experimental import pallas as pl
from jax.experimental.pallas import tpu as pltpu
from jax.sharding import PartitionSpec as P

VMEM_BYTES = 48 * 1024 * 1024


def share_kernel(target_of, i, coupling_ref, amp_ref, *refs):
    pairs = amp_ref.shape[0]
    total_pairs, offsets = coupling_ref.shape
    source = lax.axis_index("wide")
    target, wanted = target_of(source)
    row = target * pairs + i
    total = None
    for j in range(pairs):
        k = (source - target) * pairs + j - i + (offsets - 1) // 2
        valid = wanted & (k >= 0) & (k < offsets) & (row >= 0) & (row < total_pairs)
        weight = coupling_ref[jnp.clip(row, 0, total_pairs - 1), jnp.clip(k, 0, offsets - 1)]
        weight = jnp.where(valid, weight, 0.0)
        term = weight * amp_ref[j].astype(jnp.float32)
        total = term if total is None else total + term
    for more in refs[:-1]:
        total = total + more[...].astype(jnp.float32)
    refs[-1][...] = total.astype(jnp.bfloat16)


def share(coupling, target_of, i, amplitudes, arrived):
    pairs, rows, width = amplitudes.shape
    step = min(rows, 64)
    flat = pl.BlockSpec((step, width), lambda r: (r, 0))
    return pl.pallas_call(
        functools.partial(share_kernel, target_of, i),
        grid=(rows // step,),
        in_specs=[
            pl.BlockSpec(memory_space=pltpu.SMEM),
            pl.BlockSpec((pairs, step, width), lambda r: (0, r, 0)),
        ]
        + [flat] * len(arrived),
        out_specs=flat,
        out_shape=jax.ShapeDtypeStruct((rows, width), jnp.bfloat16),
        compiler_params=pltpu.CompilerParams(vmem_limit_bytes=VMEM_BYTES),
        cost_estimate=pl.CostEstimate(
            flops=2 * pairs * rows * width,
            bytes_accessed=2 * (pairs + 1 + len(arrived)) * rows * width,
            transcendentals=0,
        ),
        name="share",
    )(coupling, amplitudes, *arrived)


def cycle_kernel(mixed_ref, int_ref, out_ref):
    out_ref[0] = jnp.dot(
        mixed_ref[...], int_ref[...], preferred_element_type=jnp.float32
    ).astype(jnp.bfloat16)


def cycle_of(mixed, integrals, count):
    rows, width = mixed.shape
    part = width // count
    return pl.pallas_call(
        cycle_kernel,
        grid=(count,),
        in_specs=[
            pl.BlockSpec((rows, width), lambda n: (0, 0)),
            pl.BlockSpec((width, part), lambda n: (0, n)),
        ],
        out_specs=pl.BlockSpec((1, rows, part), lambda n: (n, 0, 0)),
        out_shape=jax.ShapeDtypeStruct((count, rows, part), jnp.bfloat16),
        compiler_params=pltpu.CompilerParams(vmem_limit_bytes=VMEM_BYTES),
        cost_estimate=pl.CostEstimate(
            flops=2 * rows * width * width,
            bytes_accessed=2 * (width * width + 2 * rows * width),
            transcendentals=0,
        ),
        name="cycle",
    )(mixed, integrals)


def update_kernel(slot, pair_ref, cyc_ref, swap_ref, erow_ref, ecol_ref, lrow_ref, mcol_ref, *refs):
    out_ref = refs[-1]
    rows, part = cyc_ref.shape[1], cyc_ref.shape[2]
    swapped = swap_ref[0].astype(jnp.float32).T
    residual = cyc_ref[0].astype(jnp.float32) + swapped
    denom = erow_ref[...] + ecol_ref[...] - pair_ref[0]
    ratio = residual / denom * lrow_ref[...]
    for t in range(rows // slot):
        out_ref[0, t * slot : (t + 1) * slot, :] = (
            ratio[t * slot : (t + 1) * slot, :] * mcol_ref[t : t + 1, :]
        ).astype(jnp.bfloat16)


def update_of(index, pairs, slot, pair, cycle, swapped, erow, ecol, lrow, mcol, before):
    count, rows, part = cycle.shape
    width = count * part
    tiles = mcol.shape[0]
    block = pl.BlockSpec((1, rows, part), lambda n: (n, 0, 0))
    column = pl.BlockSpec((rows, 1), lambda n: (0, 0))
    extra = [] if before is None else [before]
    return pl.pallas_call(
        functools.partial(update_kernel, slot),
        grid=(count,),
        in_specs=[
            pl.BlockSpec(memory_space=pltpu.SMEM),
            block,
            block,
            column,
            pl.BlockSpec((1, part), lambda n: (0, n)),
            column,
            pl.BlockSpec((tiles, part), lambda n: (0, n)),
        ]
        + [pl.BlockSpec(memory_space=pl.ANY)] * len(extra),
        out_specs=pl.BlockSpec((1, rows, part), lambda n: (index, 0, n)),
        out_shape=jax.ShapeDtypeStruct((pairs, rows, width), jnp.bfloat16),
        input_output_aliases={7: 0} if extra else {},
        compiler_params=pltpu.CompilerParams(vmem_limit_bytes=VMEM_BYTES),
        cost_estimate=pl.CostEstimate(
            flops=10 * rows * width, bytes_accessed=6 * rows * width, transcendentals=0
        ),
        name="update",
    )(pair, cycle, swapped, erow, ecol, lrow, mcol, *extra)


MESH = pl.DeviceIdType.MESH
STRIP = 16


def square_kernel(slot, coupling_ref, pair_ref, size_ref, blocks_ref, amp_ref, int_ref, energy_ref,
                  out_ref, held, passed, relayed, sent, landed, mixed, cyc, swap, erow,
                  own_sem, right_send, right_recv, left_send, left_recv, core_send, core_recv, piece_send, piece_recv, core2_send, core2_recv,
                  pass_send, pass_recv, side_send, side_recv, turn_send, turn_recv, keep_sem):
    pairs, rows, width = amp_ref.shape
    total_pairs, offsets = coupling_ref.shape
    count = width // rows
    chips = count // 2
    w, m = lax.axis_index("wide"), lax.axis_index("perm")
    z, c = m // 2, lax.rem(m, 2)
    twin = m + 1 - 2 * c
    beside = w + 1 - 2 * lax.rem(w, 2)
    above = lax.rem(w + 2, 4)
    inner = (w == 1) | (w == 2)
    outer = (w == 0) | (w == 3)
    edge = rows // STRIP * 5 // 16 * STRIP
    most = rows - edge
    z_from = jnp.where(inner, edge, 0)
    give_from = jnp.where(inner, most, 0)
    lack_from = jnp.where(inner, 0, most)
    friend = jnp.where(inner, beside, above)
    lasts = chips - 1
    half = rows // 2
    chunks = 2 * pairs

    def lines(q):
        return pl.ds(q % 2 * half, half)

    barrier = pltpu.get_barrier_semaphore()
    for k in range(1, count):
        pl.semaphore_signal(barrier, inc=1, device_id={"perm": lax.rem(m + k, count)}, device_id_type=MESH)
    for other in (beside, above):
        pl.semaphore_signal(barrier, inc=1, device_id={"wide": other}, device_id_type=MESH)
    pl.semaphore_wait(barrier, count + 1)

    def block(index):
        return held.at[pl.ds(pl.multiple_of(index * rows, rows), rows)]

    def move(src, dst, send, recv, where):
        return pltpu.make_async_remote_copy(
            src_ref=src, dst_ref=dst, send_sem=send, recv_sem=recv, device_id=where, device_id_type=MESH
        )

    def part(index, start, size):
        return held.at[pl.ds(pl.multiple_of(index * rows + start, STRIP), size)]

    def right(b, t):
        here = part(b * 2 + c, z_from, most)
        return move(here, here, right_send.at[t], right_recv.at[t], {"perm": m + 2})

    def left(b, t):
        here = part(b * 2 + c, z_from, most)
        return move(here, here, left_send.at[t], left_recv.at[t], {"perm": m - 2})

    def own_across(core):
        here = block(z * 2 + core)
        return move(here, here, core_send.at[0], core_recv.at[0], {"perm": twin})

    def across(b, core, u):
        here = part(b * 2 + core, z_from, most)
        return move(here, here, core_send.at[1 + u], core_recv.at[1 + u], {"perm": twin})

    def piece(b, start, u):
        here = part(b * 2 + c, start, edge)
        return move(here, here, piece_send.at[u], piece_recv.at[u], {"wide": friend})

    def piece_across(b, core, u):
        here = part(b * 2 + core, lack_from, edge)
        return move(here, here, core2_send.at[u], core2_recv.at[u], {"perm": twin})

    def arrivals(t, action):
        @pl.when(z - 1 - t >= 0)
        def _():
            action(z - 1 - t, t)

        @pl.when(z + 1 + t < chips)
        def _():
            action(z + 1 + t, lasts + t)

    def relay(q):
        return move(passed.at[q // 2, lines(q)], relayed.at[q // 2, lines(q)], pass_send.at[q], pass_recv.at[q], {"wide": above})

    def side(q):
        return move(sent.at[q // 2, lines(q)], landed.at[q // 2, lines(q)], side_send.at[q], side_recv.at[q], {"wide": beside})

    def turn(q, s, source):
        return move(cyc.at[q // 2, s, lines(q)], swap.at[q // 2, source, lines(q)],
                    turn_send.at[q, s], turn_recv.at[q, source], {"perm": s})

    def spread(t):
        @pl.when((z - t >= 0) & (z + 1 < chips))
        def _():
            right(z - t, t).start()

        @pl.when((z + t < chips) & (z >= 1))
        def _():
            left(z + t, t).start()

    def gather_step(t):
        @pl.when(z - 1 - t >= 0)
        def _():
            right(z - 1 - t, t).wait_recv()

        @pl.when(z + 1 + t < chips)
        def _():
            left(z + 1 + t, t).wait_recv()

        if t + 1 < lasts:
            spread(t + 1)

        def pass_on(b, u):
            piece(b, give_from, u).start()
            across(b, c, u).start()

        arrivals(t, pass_on)

    def piece_step(t):
        def pass_on(b, u):
            piece(b, lack_from, u).wait_recv()
            piece_across(b, c, u).start()

        arrivals(t, pass_on)

    def gather_end():
        own_across(1 - c).wait_recv()

        def finish(b, u):
            across(b, 1 - c, u).wait_recv()
            piece_across(b, 1 - c, u).wait_recv()

        for t in range(lasts):
            arrivals(t, finish)

    def add_up(target, q, dst, extra):
        i = q // 2
        row = target * pairs + i
        weights = []
        for j in range(pairs):
            k = (w - target) * pairs + j - i + (offsets - 1) // 2
            valid = (k >= 0) & (k < offsets)
            weights.append(jnp.where(valid, coupling_ref[row, jnp.clip(k, 0, offsets - 1)], 0.0))

        @pl.loop(q % 2 * (half // STRIP), (q % 2 + 1) * (half // STRIP))
        def _(r):
            strip = pl.ds(pl.multiple_of(r * STRIP, STRIP), STRIP)
            total = weights[0] * amp_ref[0, strip, :].astype(jnp.float32)
            for j in range(1, pairs):
                total = total + weights[j] * amp_ref[j, strip, :].astype(jnp.float32)
            if extra is not None:
                total = total + extra[i, strip, :].astype(jnp.float32)
            dst[i, strip, :] = total.astype(jnp.bfloat16)

    def side_inner(q):
        @pl.when(inner)
        def _():
            add_up(beside, q, sent, None)
            side(q).start()

    def side_outer(q):
        @pl.when(outer)
        def _():
            relay(q).wait_recv()
            add_up(beside, q, sent, relayed)
            side(q).start()

    def relay_step(q):
        @pl.when(inner)
        def _():
            if q > 1:
                relay(q - 2).wait_send()
            relay(q).start()

    def mix_step(q):
        side(q).wait_recv()
        add_up(w, q, mixed, landed)

    def kept(q):
        return pltpu.make_async_copy(
            cyc.at[q // 2, m, lines(q)], swap.at[q // 2, m, lines(q)], keep_sem.at[q]
        )

    def cycle_step(q):
        @pl.loop(1, count + 1)
        def _(k):
            s = lax.rem(m + k, count)
            columns = pl.ds(pl.multiple_of(s * rows, rows), rows)
            cyc[q // 2, s, lines(q)] = jnp.dot(
                mixed[q // 2, lines(q)], held[:, columns], preferred_element_type=jnp.float32
            ).astype(jnp.bfloat16)

            @pl.when(s != m)
            def _():
                turn(q, s, m).start()

        kept(q).start()

    def update_step(i):
        for q in (2 * i, 2 * i + 1):
            kept(q).wait()
            for k in range(1, count):
                s = lax.rem(m + k, count)
                turn(q, s, s).wait_recv()

        @pl.loop(0, count)
        def _(s):
            columns = pl.ds(pl.multiple_of(s * rows, rows), rows)
            residual = cyc[i, s].astype(jnp.float32) + swap[i, s].astype(jnp.float32).T
            denom = erow[...] + (energy_ref[:, columns] - pair_ref[i])
            ratio = residual / denom
            across_at = lax.broadcasted_iota(jnp.int32, (slot, slot), 1)
            down_at = lax.broadcasted_iota(jnp.int32, (slot, slot), 0)
            for t in range(rows // slot):
                for u in range(rows // slot):
                    row_tile = m * (rows // slot) + t
                    column_tile = s * (rows // slot) + u
                    wanted = blocks_ref[i, row_tile, column_tile].astype(jnp.float32)
                    live = (down_at < size_ref[row_tile]) & (across_at < size_ref[column_tile])
                    tile = ratio[t * slot : (t + 1) * slot, u * slot : (u + 1) * slot]
                    place = pl.ds(pl.multiple_of(s * rows + u * slot, slot), slot)
                    out_ref[i, t * slot : (t + 1) * slot, place] = jnp.where(
                        live, tile * wanted, 0.0
                    ).astype(jnp.bfloat16)

    keep = pltpu.make_async_copy(int_ref, block(m), own_sem)
    keep.start()
    keep.wait()
    spread(0)
    own_across(c).start()
    for q in range(chunks):
        @pl.when(inner)
        def _():
            add_up(3 - w, q, passed, None)

        if q == 0:
            relay_step(0)
            side_inner(0)
    relay_step(1)
    mine = energy_ref[:, pl.ds(pl.multiple_of(m * rows, rows), rows)]
    erow[...] = jnp.broadcast_to(mine, (rows, rows)).T

    gathered = begun = 0
    for q in range(chunks):
        while gathered < min(lasts, (q + 1) * 3 // 4):
            gather_step(gathered)
            if gathered > 0:
                piece_step(gathered - 1)
            gathered += 1
        side_outer(q)
        if q + 1 < chunks:
            side_inner(q + 1)
        if q + 2 < chunks:
            relay_step(q + 2)
        if gathered == lasts and begun < q - 1:
            if begun == 0:
                piece_step(lasts - 1)
                gather_end()
            while begun < q - 1:
                mix_step(begun)
                cycle_step(begun)
                begun += 1
    while gathered < lasts:
        gather_step(gathered)
        if gathered > 0:
            piece_step(gathered - 1)
        gathered += 1
    if begun == 0:
        piece_step(lasts - 1)
        gather_end()
    while begun < chunks:
        mix_step(begun)
        cycle_step(begun)
        begun += 1
    for i in range(pairs):
        update_step(i)

    own_across(c).wait_send()

    def all_gone(b, u):
        piece(b, give_from, u).wait_send()
        across(b, c, u).wait_send()
        piece_across(b, c, u).wait_send()

    for t in range(lasts):
        @pl.when((z - t >= 0) & (z + 1 < chips))
        def _():
            right(z - t, t).wait_send()

        @pl.when((z + t < chips) & (z >= 1))
        def _():
            left(z + t, t).wait_send()

        arrivals(t, all_gone)

    @pl.when(inner)
    def _():
        relay(chunks - 2).wait_send()
        relay(chunks - 1).wait_send()

    for q in range(chunks):
        side(q).wait_send()
        for k in range(1, count):
            turn(q, lax.rem(m + k, count), m).wait_send()


def square_call(slot, coupling, pair_energy, tile_sizes, blocks, amplitudes, integrals, energy):
    pairs, rows, width = amplitudes.shape
    count = width // rows
    chips = count // 2
    smem = pl.BlockSpec(memory_space=pltpu.SMEM)
    vmem = pl.BlockSpec(memory_space=pltpu.VMEM)
    anywhere = pl.BlockSpec(memory_space=pl.ANY)
    dma = pltpu.SemaphoreType.DMA
    matrices = pltpu.VMEM((pairs, rows, width), jnp.bfloat16)
    squares = pltpu.VMEM((pairs, count, rows, rows), jnp.bfloat16)
    return pl.pallas_call(
        functools.partial(square_kernel, slot),
        in_specs=[smem, smem, smem, smem, vmem, anywhere, vmem],
        out_specs=vmem,
        out_shape=jax.ShapeDtypeStruct((pairs, rows, width), jnp.bfloat16),
        scratch_shapes=[
            pltpu.VMEM((width, width), jnp.bfloat16),
            matrices, matrices, matrices, matrices, matrices,
            squares, squares,
            pltpu.VMEM((rows, rows), jnp.float32),
            dma,
            dma((chips - 1,)), dma((chips - 1,)), dma((chips - 1,)), dma((chips - 1,)),
            dma((2 * chips - 1,)), dma((2 * chips - 1,)),
            dma((2 * chips - 2,)), dma((2 * chips - 2,)), dma((2 * chips - 2,)), dma((2 * chips - 2,)),
            dma((2 * pairs,)), dma((2 * pairs,)), dma((2 * pairs,)), dma((2 * pairs,)),
            dma((2 * pairs, count)), dma((2 * pairs, count)),
            dma((2 * pairs,)),
        ],
        compiler_params=pltpu.CompilerParams(
            collective_id=0, has_side_effects=True, vmem_limit_bytes=56 * 1024 * 1024
        ),
        name="square",
    )(coupling, pair_energy, tile_sizes, blocks, amplitudes, integrals, energy)


def to_self(w):
    return w, w >= 0


def to_next(w):
    return w + 1, w >= 0


def to_last(w):
    return w - 1, w >= 0


def after(value, earlier):
    return value if earlier is None else lax.optimization_barrier((value, earlier))[0]


def per_device(amplitudes, integrals, coupling, pair_energy, virtual_energy, tile_sizes, blocks):
    pairs, rows, width = amplitudes.shape
    wide, count = lax.axis_size("wide"), lax.axis_size("perm")
    m = lax.axis_index("perm")

    tiles = tile_sizes.shape[0]
    slot = width // tiles
    if wide == 4 and count % 2 == 0 and count * rows == width and rows % slot == 0:
        return square_call(
            slot, coupling, pair_energy, tile_sizes, blocks, amplitudes, integrals, virtual_energy[None, :]
        )

    live = (jnp.arange(slot)[None, :] < tile_sizes[:, None]).reshape(width).astype(jnp.float32)
    start = m * rows
    lrow = lax.dynamic_slice_in_dim(live, start, rows, 0)[:, None]
    erow = lax.dynamic_slice_in_dim(virtual_energy, start, rows, 0)[:, None]
    ecol = virtual_energy[None, :]
    here = lax.dynamic_slice_in_dim(blocks, start // slot, rows // slot, 1).astype(jnp.float32)
    mcol = jnp.repeat(here, slot, axis=2) * live[None, None, :]

    full = lax.all_gather(integrals, "perm", axis=0, tiled=True)
    up = [(s, s + 1) for s in range(wide - 1)]
    down = [(s + 1, s) for s in range(wide - 1)]
    first = second = None
    mixed = []
    for i in range(pairs):
        term = after(share(coupling, to_next, i, amplitudes, []), first)
        first = lax.ppermute(term, "wide", up)
        term = after(share(coupling, to_last, i, amplitudes, []), second)
        second = lax.ppermute(term, "wide", down)
        arrived = [first, second]
        mixed.append(share(coupling, to_self, i, amplitudes, arrived))
    result = None
    swapped = None
    for i in range(pairs):
        cycle = cycle_of(mixed[i], full, count)
        swapped = lax.all_to_all(after(cycle, swapped), "perm", split_axis=0, concat_axis=0)
        result = update_of(
            i, pairs, slot, pair_energy[i : i + 1], cycle, swapped, erow, ecol, lrow, mcol[i], result
        )
    return result


def solution(mesh):
    in_specs = (
        P("wide", "perm", None),
        P("perm", None),
        P(),
        P("wide"),
        P(),
        P(),
        P("wide", None, None),
    )
    out_specs = P("wide", "perm", None)
    return jax.shard_map(
        per_device, mesh=mesh, in_specs=in_specs, out_specs=out_specs, check_vma=False
    )
```

```python
import functools

import jax
import jax.numpy as jnp
from jax import lax
from jax.experimental import pallas as pl
from jax.experimental.pallas import tpu as pltpu
from jax.sharding import PartitionSpec as P

VMEM_BYTES = 48 * 1024 * 1024


def share_kernel(target_of, i, coupling_ref, amp_ref, *refs):
    pairs = amp_ref.shape[0]
    total_pairs, offsets = coupling_ref.shape
    source = lax.axis_index("wide")
    target, wanted = target_of(source)
    row = target * pairs + i
    total = None
    for j in range(pairs):
        k = (source - target) * pairs + j - i + (offsets - 1) // 2
        valid = wanted & (k >= 0) & (k < offsets) & (row >= 0) & (row < total_pairs)
        weight = coupling_ref[jnp.clip(row, 0, total_pairs - 1), jnp.clip(k, 0, offsets - 1)]
        weight = jnp.where(valid, weight, 0.0)
        term = weight * amp_ref[j].astype(jnp.float32)
        total = term if total is None else total + term
    for more in refs[:-1]:
        total = total + more[...].astype(jnp.float32)
    refs[-1][...] = total.astype(jnp.bfloat16)


def share(coupling, target_of, i, amplitudes, arrived):
    pairs, rows, width = amplitudes.shape
    step = min(rows, 64)
    flat = pl.BlockSpec((step, width), lambda r: (r, 0))
    return pl.pallas_call(
        functools.partial(share_kernel, target_of, i),
        grid=(rows // step,),
        in_specs=[
            pl.BlockSpec(memory_space=pltpu.SMEM),
            pl.BlockSpec((pairs, step, width), lambda r: (0, r, 0)),
        ]
        + [flat] * len(arrived),
        out_specs=flat,
        out_shape=jax.ShapeDtypeStruct((rows, width), jnp.bfloat16),
        compiler_params=pltpu.CompilerParams(vmem_limit_bytes=VMEM_BYTES),
        cost_estimate=pl.CostEstimate(
            flops=2 * pairs * rows * width,
            bytes_accessed=2 * (pairs + 1 + len(arrived)) * rows * width,
            transcendentals=0,
        ),
        name="share",
    )(coupling, amplitudes, *arrived)


def cycle_kernel(mixed_ref, int_ref, out_ref):
    out_ref[0] = jnp.dot(
        mixed_ref[...], int_ref[...], preferred_element_type=jnp.float32
    ).astype(jnp.bfloat16)


def cycle_of(mixed, integrals, count):
    rows, width = mixed.shape
    part = width // count
    return pl.pallas_call(
        cycle_kernel,
        grid=(count,),
        in_specs=[
            pl.BlockSpec((rows, width), lambda n: (0, 0)),
            pl.BlockSpec((width, part), lambda n: (0, n)),
        ],
        out_specs=pl.BlockSpec((1, rows, part), lambda n: (n, 0, 0)),
        out_shape=jax.ShapeDtypeStruct((count, rows, part), jnp.bfloat16),
        compiler_params=pltpu.CompilerParams(vmem_limit_bytes=VMEM_BYTES),
        cost_estimate=pl.CostEstimate(
            flops=2 * rows * width * width,
            bytes_accessed=2 * (width * width + 2 * rows * width),
            transcendentals=0,
        ),
        name="cycle",
    )(mixed, integrals)


def update_kernel(slot, pair_ref, cyc_ref, swap_ref, erow_ref, ecol_ref, lrow_ref, mcol_ref, *refs):
    out_ref = refs[-1]
    rows, part = cyc_ref.shape[1], cyc_ref.shape[2]
    swapped = swap_ref[0].astype(jnp.float32).T
    residual = cyc_ref[0].astype(jnp.float32) + swapped
    denom = erow_ref[...] + ecol_ref[...] - pair_ref[0]
    ratio = residual / denom * lrow_ref[...]
    for t in range(rows // slot):
        out_ref[0, t * slot : (t + 1) * slot, :] = (
            ratio[t * slot : (t + 1) * slot, :] * mcol_ref[t : t + 1, :]
        ).astype(jnp.bfloat16)


def update_of(index, pairs, slot, pair, cycle, swapped, erow, ecol, lrow, mcol, before):
    count, rows, part = cycle.shape
    width = count * part
    tiles = mcol.shape[0]
    block = pl.BlockSpec((1, rows, part), lambda n: (n, 0, 0))
    column = pl.BlockSpec((rows, 1), lambda n: (0, 0))
    extra = [] if before is None else [before]
    return pl.pallas_call(
        functools.partial(update_kernel, slot),
        grid=(count,),
        in_specs=[
            pl.BlockSpec(memory_space=pltpu.SMEM),
            block,
            block,
            column,
            pl.BlockSpec((1, part), lambda n: (0, n)),
            column,
            pl.BlockSpec((tiles, part), lambda n: (0, n)),
        ]
        + [pl.BlockSpec(memory_space=pl.ANY)] * len(extra),
        out_specs=pl.BlockSpec((1, rows, part), lambda n: (index, 0, n)),
        out_shape=jax.ShapeDtypeStruct((pairs, rows, width), jnp.bfloat16),
        input_output_aliases={7: 0} if extra else {},
        compiler_params=pltpu.CompilerParams(vmem_limit_bytes=VMEM_BYTES),
        cost_estimate=pl.CostEstimate(
            flops=10 * rows * width, bytes_accessed=6 * rows * width, transcendentals=0
        ),
        name="update",
    )(pair, cycle, swapped, erow, ecol, lrow, mcol, *extra)


MESH = pl.DeviceIdType.MESH
STRIP = 16


def square_kernel(slot, coupling_ref, pair_ref, size_ref, blocks_ref, amp_ref, int_ref, energy_ref,
                  out_ref, held, passed, relayed, sent, landed, mixed, cyc, swap, erow,
                  own_sem, right_send, right_recv, left_send, left_recv, core_send, core_recv, piece_send, piece_recv, core2_send, core2_recv,
                  pass_send, pass_recv, side_send, side_recv, turn_send, turn_recv, keep_sem):
    pairs, rows, width = amp_ref.shape
    total_pairs, offsets = coupling_ref.shape
    count = width // rows
    chips = count // 2
    w, m = lax.axis_index("wide"), lax.axis_index("perm")
    z, c = m // 2, lax.rem(m, 2)
    twin = m + 1 - 2 * c
    beside = w + 1 - 2 * lax.rem(w, 2)
    above = lax.rem(w + 2, 4)
    inner = (w == 1) | (w == 2)
    outer = (w == 0) | (w == 3)
    edge = rows // STRIP * 5 // 16 * STRIP
    most = rows - edge
    z_from = jnp.where(inner, edge, 0)
    give_from = jnp.where(inner, most, 0)
    lack_from = jnp.where(inner, 0, most)
    friend = jnp.where(inner, beside, above)
    lasts = chips - 1
    half = rows // 2
    chunks = 2 * pairs

    def lines(q):
        return pl.ds(q % 2 * half, half)

    barrier = pltpu.get_barrier_semaphore()
    for k in range(1, count):
        pl.semaphore_signal(barrier, inc=1, device_id={"perm": lax.rem(m + k, count)}, device_id_type=MESH)
    for other in (beside, above):
        pl.semaphore_signal(barrier, inc=1, device_id={"wide": other}, device_id_type=MESH)
    pl.semaphore_wait(barrier, count + 1)

    def block(index):
        return held.at[pl.ds(pl.multiple_of(index * rows, rows), rows)]

    def move(src, dst, send, recv, where):
        return pltpu.make_async_remote_copy(
            src_ref=src, dst_ref=dst, send_sem=send, recv_sem=recv, device_id=where, device_id_type=MESH
        )

    def part(index, start, size):
        return held.at[pl.ds(pl.multiple_of(index * rows + start, STRIP), size)]

    def right(b, t):
        here = part(b * 2 + c, z_from, most)
        return move(here, here, right_send.at[t], right_recv.at[t], {"perm": m + 2})

    def left(b, t):
        here = part(b * 2 + c, z_from, most)
        return move(here, here, left_send.at[t], left_recv.at[t], {"perm": m - 2})

    def own_across(core):
        here = block(z * 2 + core)
        return move(here, here, core_send.at[0], core_recv.at[0], {"perm": twin})

    def across(b, core, u):
        here = part(b * 2 + core, z_from, most)
        return move(here, here, core_send.at[1 + u], core_recv.at[1 + u], {"perm": twin})

    def piece(b, start, u):
        here = part(b * 2 + c, start, edge)
        return move(here, here, piece_send.at[u], piece_recv.at[u], {"wide": friend})

    def piece_across(b, core, u):
        here = part(b * 2 + core, lack_from, edge)
        return move(here, here, core2_send.at[u], core2_recv.at[u], {"perm": twin})

    def arrivals(t, action):
        @pl.when(z - 1 - t >= 0)
        def _():
            action(z - 1 - t, t)

        @pl.when(z + 1 + t < chips)
        def _():
            action(z + 1 + t, lasts + t)

    def relay(q):
        return move(passed.at[q // 2, lines(q)], relayed.at[q // 2, lines(q)], pass_send.at[q], pass_recv.at[q], {"wide": above})

    def side(q):
        return move(sent.at[q // 2, lines(q)], landed.at[q // 2, lines(q)], side_send.at[q], side_recv.at[q], {"wide": beside})

    def turn(q, s, source):
        return move(cyc.at[q // 2, s, lines(q)], swap.at[q // 2, source, lines(q)],
                    turn_send.at[q, s], turn_recv.at[q, source], {"perm": s})

    def spread(t):
        @pl.when((z - t >= 0) & (z + 1 < chips))
        def _():
            right(z - t, t).start()

        @pl.when((z + t < chips) & (z >= 1))
        def _():
            left(z + t, t).start()

    def gather_step(t):
        @pl.when(z - 1 - t >= 0)
        def _():
            right(z - 1 - t, t).wait_recv()

        @pl.when(z + 1 + t < chips)
        def _():
            left(z + 1 + t, t).wait_recv()

        if t + 1 < lasts:
            spread(t + 1)

        def pass_on(b, u):
            piece(b, give_from, u).start()
            across(b, c, u).start()

        arrivals(t, pass_on)

    def piece_step(t):
        def pass_on(b, u):
            piece(b, lack_from, u).wait_recv()
            piece_across(b, c, u).start()

        arrivals(t, pass_on)

    def gather_end():
        own_across(1 - c).wait_recv()

        def finish(b, u):
            across(b, 1 - c, u).wait_recv()
            piece_across(b, 1 - c, u).wait_recv()

        for t in range(lasts):
            arrivals(t, finish)

    def add_up(target, q, dst, extra):
        i = q // 2
        row = target * pairs + i
        weights = []
        for j in range(pairs):
            k = (w - target) * pairs + j - i + (offsets - 1) // 2
            valid = (k >= 0) & (k < offsets)
            weights.append(jnp.where(valid, coupling_ref[row, jnp.clip(k, 0, offsets - 1)], 0.0))

        @pl.loop(q % 2 * (half // STRIP), (q % 2 + 1) * (half // STRIP))
        def _(r):
            strip = pl.ds(pl.multiple_of(r * STRIP, STRIP), STRIP)
            total = weights[0] * amp_ref[0, strip, :].astype(jnp.float32)
            for j in range(1, pairs):
                total = total + weights[j] * amp_ref[j, strip, :].astype(jnp.float32)
            if extra is not None:
                total = total + extra[i, strip, :].astype(jnp.float32)
            dst[i, strip, :] = total.astype(jnp.bfloat16)

    def side_inner(q):
        @pl.when(inner)
        def _():
            add_up(beside, q, sent, None)
            side(q).start()

    def side_outer(q):
        @pl.when(outer)
        def _():
            relay(q).wait_recv()
            add_up(beside, q, sent, relayed)
            side(q).start()

    def relay_step(q):
        @pl.when(inner)
        def _():
            if q > 1:
                relay(q - 2).wait_send()
            relay(q).start()

    def mix_step(q):
        side(q).wait_recv()
        add_up(w, q, mixed, landed)

    def kept(q):
        return pltpu.make_async_copy(
            cyc.at[q // 2, m, lines(q)], swap.at[q // 2, m, lines(q)], keep_sem.at[q]
        )

    def cycle_step(q):
        @pl.loop(0, count)
        def _(k):
            near = k // chips
            s = lax.rem(m // chips + 1 - near, 2) * chips + lax.rem(m + k + near, chips)
            columns = pl.ds(pl.multiple_of(s * rows, rows), rows)
            cyc[q // 2, s, lines(q)] = jnp.dot(
                mixed[q // 2, lines(q)], held[:, columns], preferred_element_type=jnp.float32
            ).astype(jnp.bfloat16)

            @pl.when(s != m)
            def _():
                turn(q, s, m).start()

        kept(q).start()

    def update_step(i):
        for q in (2 * i, 2 * i + 1):
            kept(q).wait()
            for k in range(1, count):
                s = lax.rem(m + k, count)
                turn(q, s, s).wait_recv()

        @pl.loop(0, count)
        def _(s):
            columns = pl.ds(pl.multiple_of(s * rows, rows), rows)
            residual = cyc[i, s].astype(jnp.float32) + swap[i, s].astype(jnp.float32).T
            denom = erow[...] + (energy_ref[:, columns] - pair_ref[i])
            ratio = residual / denom
            across_at = lax.broadcasted_iota(jnp.int32, (slot, slot), 1)
            down_at = lax.broadcasted_iota(jnp.int32, (slot, slot), 0)
            for t in range(rows // slot):
                for u in range(rows // slot):
                    row_tile = m * (rows // slot) + t
                    column_tile = s * (rows // slot) + u
                    wanted = blocks_ref[i, row_tile, column_tile].astype(jnp.float32)
                    live = (down_at < size_ref[row_tile]) & (across_at < size_ref[column_tile])
                    tile = ratio[t * slot : (t + 1) * slot, u * slot : (u + 1) * slot]
                    place = pl.ds(pl.multiple_of(s * rows + u * slot, slot), slot)
                    out_ref[i, t * slot : (t + 1) * slot, place] = jnp.where(
                        live, tile * wanted, 0.0
                    ).astype(jnp.bfloat16)

    keep = pltpu.make_async_copy(int_ref, block(m), own_sem)
    keep.start()
    keep.wait()
    spread(0)
    own_across(c).start()
    for q in range(chunks):
        @pl.when(inner)
        def _():
            add_up(3 - w, q, passed, None)

        if q == 0:
            relay_step(0)
            side_inner(0)
    relay_step(1)
    mine = energy_ref[:, pl.ds(pl.multiple_of(m * rows, rows), rows)]
    erow[...] = jnp.broadcast_to(mine, (rows, rows)).T

    gathered = begun = 0
    for q in range(chunks):
        while gathered < min(lasts, (q + 1) * 3 // 4):
            gather_step(gathered)
            if gathered > 0:
                piece_step(gathered - 1)
            gathered += 1
        side_outer(q)
        if q + 1 < chunks:
            side_inner(q + 1)
        if q + 2 < chunks:
            relay_step(q + 2)
        if gathered == lasts and begun < q - 1:
            if begun == 0:
                piece_step(lasts - 1)
                gather_end()
            while begun < q - 1:
                mix_step(begun)
                cycle_step(begun)
                begun += 1
    while gathered < lasts:
        gather_step(gathered)
        if gathered > 0:
            piece_step(gathered - 1)
        gathered += 1
    if begun == 0:
        piece_step(lasts - 1)
        gather_end()
    while begun < chunks:
        mix_step(begun)
        cycle_step(begun)
        begun += 1
    for i in range(pairs):
        update_step(i)

    own_across(c).wait_send()

    def all_gone(b, u):
        piece(b, give_from, u).wait_send()
        across(b, c, u).wait_send()
        piece_across(b, c, u).wait_send()

    for t in range(lasts):
        @pl.when((z - t >= 0) & (z + 1 < chips))
        def _():
            right(z - t, t).wait_send()

        @pl.when((z + t < chips) & (z >= 1))
        def _():
            left(z + t, t).wait_send()

        arrivals(t, all_gone)

    @pl.when(inner)
    def _():
        relay(chunks - 2).wait_send()
        relay(chunks - 1).wait_send()

    for q in range(chunks):
        side(q).wait_send()
        for k in range(1, count):
            turn(q, lax.rem(m + k, count), m).wait_send()


def square_call(slot, coupling, pair_energy, tile_sizes, blocks, amplitudes, integrals, energy):
    pairs, rows, width = amplitudes.shape
    count = width // rows
    chips = count // 2
    smem = pl.BlockSpec(memory_space=pltpu.SMEM)
    vmem = pl.BlockSpec(memory_space=pltpu.VMEM)
    anywhere = pl.BlockSpec(memory_space=pl.ANY)
    dma = pltpu.SemaphoreType.DMA
    matrices = pltpu.VMEM((pairs, rows, width), jnp.bfloat16)
    squares = pltpu.VMEM((pairs, count, rows, rows), jnp.bfloat16)
    return pl.pallas_call(
        functools.partial(square_kernel, slot),
        in_specs=[smem, smem, smem, smem, vmem, anywhere, vmem],
        out_specs=vmem,
        out_shape=jax.ShapeDtypeStruct((pairs, rows, width), jnp.bfloat16),
        scratch_shapes=[
            pltpu.VMEM((width, width), jnp.bfloat16),
            matrices, matrices, matrices, matrices, matrices,
            squares, squares,
            pltpu.VMEM((rows, rows), jnp.float32),
            dma,
            dma((chips - 1,)), dma((chips - 1,)), dma((chips - 1,)), dma((chips - 1,)),
            dma((2 * chips - 1,)), dma((2 * chips - 1,)),
            dma((2 * chips - 2,)), dma((2 * chips - 2,)), dma((2 * chips - 2,)), dma((2 * chips - 2,)),
            dma((2 * pairs,)), dma((2 * pairs,)), dma((2 * pairs,)), dma((2 * pairs,)),
            dma((2 * pairs, count)), dma((2 * pairs, count)),
            dma((2 * pairs,)),
        ],
        compiler_params=pltpu.CompilerParams(
            collective_id=0, has_side_effects=True, vmem_limit_bytes=56 * 1024 * 1024
        ),
        name="square",
    )(coupling, pair_energy, tile_sizes, blocks, amplitudes, integrals, energy)


def to_self(w):
    return w, w >= 0


def to_next(w):
    return w + 1, w >= 0


def to_last(w):
    return w - 1, w >= 0


def after(value, earlier):
    return value if earlier is None else lax.optimization_barrier((value, earlier))[0]


def per_device(amplitudes, integrals, coupling, pair_energy, virtual_energy, tile_sizes, blocks):
    pairs, rows, width = amplitudes.shape
    wide, count = lax.axis_size("wide"), lax.axis_size("perm")
    m = lax.axis_index("perm")

    tiles = tile_sizes.shape[0]
    slot = width // tiles
    if wide == 4 and count % 2 == 0 and count * rows == width and rows % slot == 0:
        return square_call(
            slot, coupling, pair_energy, tile_sizes, blocks, amplitudes, integrals, virtual_energy[None, :]
        )

    live = (jnp.arange(slot)[None, :] < tile_sizes[:, None]).reshape(width).astype(jnp.float32)
    start = m * rows
    lrow = lax.dynamic_slice_in_dim(live, start, rows, 0)[:, None]
    erow = lax.dynamic_slice_in_dim(virtual_energy, start, rows, 0)[:, None]
    ecol = virtual_energy[None, :]
    here = lax.dynamic_slice_in_dim(blocks, start // slot, rows // slot, 1).astype(jnp.float32)
    mcol = jnp.repeat(here, slot, axis=2) * live[None, None, :]

    full = lax.all_gather(integrals, "perm", axis=0, tiled=True)
    up = [(s, s + 1) for s in range(wide - 1)]
    down = [(s + 1, s) for s in range(wide - 1)]
    first = second = None
    mixed = []
    for i in range(pairs):
        term = after(share(coupling, to_next, i, amplitudes, []), first)
        first = lax.ppermute(term, "wide", up)
        term = after(share(coupling, to_last, i, amplitudes, []), second)
        second = lax.ppermute(term, "wide", down)
        arrived = [first, second]
        mixed.append(share(coupling, to_self, i, amplitudes, arrived))
    result = None
    swapped = None
    for i in range(pairs):
        cycle = cycle_of(mixed[i], full, count)
        swapped = lax.all_to_all(after(cycle, swapped), "perm", split_axis=0, concat_axis=0)
        result = update_of(
            i, pairs, slot, pair_energy[i : i + 1], cycle, swapped, erow, ecol, lrow, mcol[i], result
        )
    return result


def solution(mesh):
    in_specs = (
        P("wide", "perm", None),
        P("perm", None),
        P(),
        P("wide"),
        P(),
        P(),
        P("wide", None, None),
    )
    out_specs = P("wide", "perm", None)
    return jax.shard_map(
        per_device, mesh=mesh, in_specs=in_specs, out_specs=out_specs, check_vma=False
    )
```
